32 devices in a mesh: tok: 8 (over z, y), mdl: 4 (over x, core).
Axes of the slice: x: 2, y: 2, z: 4, core: 2. Of those that a mesh axis runs over, the one named last changes fastest.
Arguments:
- tokens: bfloat16 [2048, 5120], P('tok'), may hold values from -32 to 32
- norm_gain: bfloat16 [5120], replicated, may hold values from 0.099609375 to 1.8984375
- w_query: bfloat16 [5120, 4096], P(None, 'mdl'), may hold values from -0.078125 to 0.078125
- w_key: bfloat16 [5120, 1024], P(None, 'mdl'), may hold values from -0.3125 to 0.3125
- w_value: bfloat16 [5120, 1024], P(None, 'mdl'), may hold values from -0.078125 to 0.078125
- w_out: bfloat16 [4096, 5120], P('mdl'), may hold values from -0.09375 to 0.09375
- prompt_keys: bfloat16 [6, 4096, 8, 128], P(None, 'tok', 'mdl'), may hold values from -6 to 6
- prompt_values: bfloat16 [6, 4096, 8, 128], P(None, 'tok', 'mdl'), may hold values from -24 to 24
- cache_keys: bfloat16 [64, 2048, 8, 128], P('tok', None, 'mdl'), may hold values from -6 to 6
- cache_values: bfloat16 [64, 2048, 8, 128], P('tok', None, 'mdl'), may hold values from -24 to 24
- cache_length: int32 [64], P('tok'), may hold values from 1 to 2048, as said below
- request_group: int32 [64], replicated, may hold values from 0 to 5
- ancestors: int32 [64, 32, 32], P('tok'), may hold values from 0 to 1, as said below
- accepted: int32 [64, 8], P('tok'), may hold values from -1 to 31, as said below
Outputs:
- attention_out: bfloat16 [2048, 5120], P('tok', 'mdl')
- compact_rows: bfloat16 [64, 8, 5120], P('tok', None, 'mdl')
The draws below stay inside these ranges and needn't reach their ends.
Inputs may be any that keep to these rules, and one draw needn't show every extreme that they name: `cache_length`: some request has exactly 2048 live slots. ancestors[r, a, b] is 1 where tree slot b is slot a itself or an ancestor of it in request r's draft tree, else 0; each tree has one root, and slots are in no particular order. Entry k of request r is the tree slot of the accepted path's node at depth k, from the root on, for k below the path's length, and -1 after it; a path holds 1 to 8 nodes, and some request's path holds 8.
All inputs are finite; a program needn't handle non-finite values.
Results may differ from the reference program's by a relative error of at most 0.017.
Values may be sent and summed in bfloat16 or wider, within the bound.
A program may use at most 192 MiB of HBM per device.

```python
import jax
import jax.numpy as jnp
from jax import lax

D = 5120
HQ = 32
KVH = 8
HD = 128
CACHE = 2048
TREE = 32
ACC = 8
PROMPT = 4096
GROUPS = 6
REQ = 64
TOKENS = 2048
N_TOK = 8


def draw_tokens(key, part):
    base = jax.random.fold_in(key, 1)
    key_rows, key_columns, key_main = jax.random.split(base, 3)
    column_scale = jnp.exp(jax.random.uniform(key_columns, (D,), jnp.float32, jnp.log(0.3), jnp.log(3.0)))
    row_scale = jnp.exp(jax.random.uniform(key_rows, (TOKENS, 1), jnp.float32, jnp.log(0.5), jnp.log(2.0)))
    values = jnp.clip(jax.random.normal(key_main, (TOKENS, D), jnp.float32), -5.0, 5.0)
    return (values * column_scale[None, :] * row_scale).astype(jnp.bfloat16)


def draw_cache_length(key, part):
    base = jax.random.fold_in(key, 3)
    key_length, key_shift, key_chosen = jax.random.split(base, 3)
    length = jax.random.randint(key_length, (REQ,), 1, CACHE + 1)
    shifts = jax.random.randint(key_shift, (REQ,), 0, 3)
    divisor = jnp.where(shifts == 0, 1, jnp.where(shifts == 1, 2, 4))
    length = jnp.maximum(length // divisor, 1)
    chosen = jax.random.randint(key_chosen, (), 0, REQ)
    return jnp.where(jnp.arange(REQ, dtype=jnp.int32) == chosen, CACHE, length).astype(jnp.int32)


def tree_tables(key):
    base = jax.random.fold_in(key, 7)
    key_order, key_parent, key_length, key_chosen = jax.random.split(base, 4)
    nodes = jnp.arange(TREE, dtype=jnp.int32)
    scores = jax.random.randint(key_order, (REQ, TREE), 0, 1 << 20) * TREE + nodes[None, :]
    slot_of = jnp.argsort(scores, axis=1).astype(jnp.int32)
    draws = jax.random.randint(key_parent, (REQ, TREE), 0, 1 << 20)
    parent = jnp.where(nodes[None, :] < ACC, nodes[None, :] - 1, draws % jnp.maximum(nodes[None, :], 1))
    ancestry = jnp.zeros((REQ, TREE, TREE), jnp.int32)
    for member in range(TREE):
        itself = jnp.broadcast_to((nodes == member).astype(jnp.int32)[None, :], (REQ, TREE))
        if member == 0:
            lineage = itself
        else:
            above = jnp.take_along_axis(ancestry, jnp.maximum(parent[:, member], 0)[:, None, None], axis=1)[:, 0, :]
            lineage = above + itself
        ancestry = ancestry.at[:, member, :].set(lineage)
    raw_of = jnp.argsort(slot_of, axis=1).astype(jnp.int32)
    first = jnp.take_along_axis(ancestry, raw_of[:, :, None], axis=1)
    table = jnp.take_along_axis(first, raw_of[:, None, :], axis=2)
    length = jax.random.randint(key_length, (REQ,), 1, ACC + 1)
    chosen = jax.random.randint(key_chosen, (), 0, REQ)
    length = jnp.where(jnp.arange(REQ, dtype=jnp.int32) == chosen, ACC, length)
    spine = slot_of[:, :ACC]
    paths = jnp.where(jnp.arange(ACC, dtype=jnp.int32)[None, :] < length[:, None], spine, -1)
    return (table.astype(jnp.int32), paths.astype(jnp.int32))


def draw_ancestors(key, part):
    return tree_tables(key)[0]


def draw_accepted(key, part):
    return tree_tables(key)[1]


def touch_ends(result, stream_key, smallest, high):
    index_at = [jax.random.randint(jax.random.fold_in(stream_key, axis), (), 0, length) for axis, length in enumerate(result.shape)]
    longest = result.shape.index(max(result.shape))
    beside = index_at[:longest] + [(index_at[longest] + 1) % result.shape[longest]] + index_at[longest + 1:]
    return result.at[tuple(index_at)].set(smallest).at[tuple(beside)].set(high)


def steps_of(own_key, extent, cuts, least, high):
    def one(dim, blocks):
        heights = jax.random.uniform(jax.random.fold_in(jax.random.fold_in(own_key, 6), dim), (blocks,), jnp.float32, least / len(cuts), high / len(cuts))
        return jnp.repeat(jnp.exp(heights), extent[dim] // blocks).reshape((-1,) + (1,) * (len(extent) - dim - 1))

    level = one(*cuts[0])
    for cut in cuts[1:]:
        level = level * one(*cut)
    return level


def normal_values(key, extent, deviation, limit, pieces=(), kind=jnp.bfloat16):
    result = deviation * jax.random.normal(key, extent, jnp.float32)
    if pieces:
        result = result * steps_of(key, extent, pieces, -0.22, 0.18)
    return jnp.clip(result, -limit, limit).astype(kind)


def setup_inputs(seed: int = 0) -> dict:
    key_list = jax.random.split(jax.random.key(seed), 15)
    tokens = draw_tokens(jax.random.fold_in(key_list[14], 71), 0)
    norm_gain = jnp.clip(1.0 + 0.18 * jax.random.normal(key_list[1], (D,), jnp.float32), 0.099609375, 1.8984375).astype(jnp.bfloat16)
    w_query = normal_values(key_list[2], (D, HQ * HD), D ** -0.5, 0.078125, ((1, 4),))
    w_key = normal_values(key_list[3], (D, KVH * HD), (D // 16) ** -0.5, 0.3125, ((1, 4),))
    w_value = normal_values(key_list[4], (D, KVH * HD), D ** -0.5, 0.078125, ((1, 4),))
    w_out = normal_values(key_list[5], (HQ * HD, D), (HQ * HD) ** -0.5, 0.09375, ((0, 4),))
    prompt_keys = normal_values(key_list[6], (GROUPS, PROMPT, KVH, HD), 1.0, 6.0, ((1, 8), (2, 4)))
    prompt_values = normal_values(key_list[7], (GROUPS, PROMPT, KVH, HD), 4.0, 24.0, ((1, 8), (2, 4)))
    cache_keys = normal_values(key_list[8], (REQ, CACHE, KVH, HD), 1.0, 6.0, ((0, 8), (2, 4)))
    cache_values = normal_values(key_list[9], (REQ, CACHE, KVH, HD), 4.0, 24.0, ((0, 8), (2, 4)))
    cache_length = draw_cache_length(jax.random.fold_in(key_list[14], 71), 0)
    request_group = touch_ends(jax.random.randint(key_list[11], (REQ,), 0, GROUPS), jax.random.fold_in(key_list[11], 1), 0, GROUPS - 1).astype(jnp.int32)
    ancestors = draw_ancestors(jax.random.fold_in(key_list[14], 71), 0)
    accepted = draw_accepted(jax.random.fold_in(key_list[14], 71), 0)
    return {"tokens": tokens, "norm_gain": norm_gain, "w_query": w_query, "w_key": w_key, "w_value": w_value, "w_out": w_out, "prompt_keys": prompt_keys, "prompt_values": prompt_values, "cache_keys": cache_keys, "cache_values": cache_values, "cache_length": cache_length, "request_group": request_group, "ancestors": ancestors, "accepted": accepted}


THETA = 100000000.0
EPS = 1e-05

def rotate_pairs(vectors, positions):
    middle = vectors.shape[-1] // 2
    exponent = jnp.arange(middle, dtype=jnp.float32) * (2.0 / vectors.shape[-1])
    inverse = jnp.power(jnp.float32(THETA), -exponent)
    angles = positions.astype(jnp.float32)[:, None] * inverse[None, :]
    cosine = jnp.cos(angles)[:, None, :]
    sine_part = jnp.sin(angles)[:, None, :]
    leading = vectors[..., :middle]
    trailing = vectors[..., middle:]
    return jnp.concatenate([leading * cosine - trailing * sine_part, trailing * cosine + leading * sine_part], axis=-1)

def round_bfloat(values):
    return lax.optimization_barrier(values.astype(jnp.bfloat16)).astype(jnp.float32)

def reference(tokens, norm_gain, w_query, w_key, w_value, w_out, prompt_keys, prompt_values, cache_keys, cache_values, cache_length, request_group, ancestors, accepted):
    wide = tokens.astype(jnp.float32)
    normed = (wide * lax.rsqrt(lax.optimization_barrier(jnp.mean(wide * wide, axis=1, keepdims=True)) + EPS) * norm_gain.astype(jnp.float32)).astype(jnp.bfloat16)
    queries = jnp.dot(normed, w_query, preferred_element_type=jnp.float32).reshape(TOKENS, HQ, HD)
    new_keys = jnp.dot(normed, w_key, preferred_element_type=jnp.float32).reshape(TOKENS, KVH, HD)
    new_values = jnp.dot(normed, w_value, preferred_element_type=jnp.float32).astype(jnp.bfloat16).reshape(REQ, TREE, KVH, HD)
    depth = lax.optimization_barrier(jnp.sum(ancestors, axis=2)) - 1
    positions = (PROMPT + cache_length[:, None] + depth).reshape(TOKENS)
    queries = rotate_pairs(queries, positions).astype(jnp.bfloat16).reshape(REQ, TREE, KVH, HQ // KVH, HD)
    new_keys = rotate_pairs(new_keys, positions).astype(jnp.bfloat16).reshape(REQ, TREE, KVH, HD)
    factor = HD ** (-0.5)
    slice_rows = PROMPT // N_TOK

    def one_request(operands):
        grouped, tree_keys, tree_values, group_index, own_keys, own_values, length, lineage = operands
        grouped = grouped.astype(jnp.float32)
        shared_keys = lax.dynamic_index_in_dim(prompt_keys, group_index, 0, keepdims=False).astype(jnp.float32).reshape(N_TOK, slice_rows, KVH, HD)
        shared_values = lax.dynamic_index_in_dim(prompt_values, group_index, 0, keepdims=False).astype(jnp.float32).reshape(N_TOK, slice_rows, KVH, HD)
        scores = jnp.einsum('tkgd,sckd->tkgsc', grouped, shared_keys) * factor
        weights = jnp.exp(scores)
        totals = lax.optimization_barrier(jnp.sum(weights, axis=4))
        numerator = jnp.einsum('tkgsc,sckd->tkgsd', round_bfloat(weights), shared_values)
        outputs = round_bfloat(numerator / totals[..., None])
        prompt_part = lax.optimization_barrier(jnp.sum(totals[..., None] * outputs, axis=3))
        prompt_total = lax.optimization_barrier(jnp.sum(totals, axis=3))
        cache_scores = jnp.einsum('tkgd,ckd->tkgc', grouped, own_keys.astype(jnp.float32)) * factor
        live = jnp.arange(CACHE, dtype=jnp.int32) < length
        cache_weights = jnp.where(live, jnp.exp(cache_scores), 0.0)
        cache_part = jnp.einsum('tkgc,ckd->tkgd', round_bfloat(cache_weights), own_values.astype(jnp.float32))
        tree_scores = jnp.einsum('tkgd,mkd->tkgm', grouped, tree_keys.astype(jnp.float32)) * factor
        tree_weights = jnp.where(lineage[:, None, None, :] > 0, jnp.exp(tree_scores), 0.0)
        tree_part = jnp.einsum('tkgm,mkd->tkgd', round_bfloat(tree_weights), tree_values.astype(jnp.float32))
        totals_all = prompt_total + lax.optimization_barrier(jnp.sum(cache_weights, axis=3)) + lax.optimization_barrier(jnp.sum(tree_weights, axis=3))
        merged = (prompt_part + cache_part + tree_part) / totals_all[..., None]
        return merged.astype(jnp.bfloat16).reshape(TREE, HQ * HD)
    attended = lax.map(one_request, (queries, new_keys, new_values, request_group, cache_keys, cache_values, cache_length, ancestors)).reshape(TOKENS, HQ * HD)
    attention_out = jnp.dot(attended, w_out, preferred_element_type=jnp.float32).astype(jnp.bfloat16)
    residual = wide + attention_out.astype(jnp.float32)
    rows_index = (jnp.arange(REQ, dtype=jnp.int32)[:, None] * TREE + jnp.maximum(accepted, 0)).reshape(REQ * ACC)
    picked = jnp.take(residual, rows_index, axis=0).reshape(REQ, ACC, D)
    compact_rows = jnp.where(accepted[:, :, None] >= 0, picked, 0.0).astype(jnp.bfloat16)
    return (attention_out, compact_rows)
```

```python
import functools
import math

import jax
import jax.numpy as jnp
from jax import lax
from jax.experimental import pallas as pl
from jax.experimental.pallas import tpu as pltpu
from jax.sharding import PartitionSpec as P

PROMPT = 4096
THETA = 100000000.0
EPS = 1e-05
PAD = 16
NEG = -1e30
CONTRACT_LAST = (((1,), (1,)), ((), ()))


def rotate_pairs(vectors, positions):
    middle = vectors.shape[-1] // 2
    exponent = jnp.arange(middle, dtype=jnp.float32) * (2.0 / vectors.shape[-1])
    inverse = jnp.power(jnp.float32(THETA), -exponent)
    angles = positions.astype(jnp.float32)[:, None] * inverse[None, :]
    cosine = jnp.cos(angles)[:, None, :]
    sine_part = jnp.sin(angles)[:, None, :]
    leading = vectors[..., :middle]
    trailing = vectors[..., middle:]
    return jnp.concatenate(
        [leading * cosine - trailing * sine_part, trailing * cosine + leading * sine_part], axis=-1
    )


def stack_heads(block, head_dim):
    count = block.shape[1] // head_dim
    return jnp.concatenate(
        [block[:, j * head_dim : (j + 1) * head_dim] for j in range(count)], axis=0
    )


def own_kernel(
    key_heads, chunk, scale, length_ref, q_ref, k_ref, v_ref, tk_ref, tv_ref, mask_ref,
    part_ref, total_ref,
):
    n = pl.program_id(0)
    tree, width = q_ref.shape
    head_dim = k_ref.shape[2]
    query = stack_heads(q_ref[...], head_dim)
    rows = query.shape[0]
    per = rows // key_heads
    live = length_ref[n] * key_heads

    scores = lax.dot_general(query, tk_ref[0], CONTRACT_LAST, preferred_element_type=jnp.float32)
    weights = jnp.exp2(jnp.where(mask_ref[0] > 0, scores * scale, NEG))
    total0 = jnp.sum(weights, axis=1, keepdims=True)
    part0 = jnp.dot(weights.astype(jnp.bfloat16), tv_ref[0], preferred_element_type=jnp.float32)
    row_head = lax.broadcasted_iota(jnp.int32, (rows, chunk), 0) // per
    column = lax.broadcasted_iota(jnp.int32, (rows, chunk), 1)
    own_head = (column % key_heads) == row_head

    def step(i, carry):
        part, total = carry
        start = pl.multiple_of(i * chunk, chunk)
        keys = k_ref[0, pl.ds(start, chunk), :]
        values = v_ref[0, pl.ds(start, chunk), :]
        scores = lax.dot_general(query, keys, CONTRACT_LAST, preferred_element_type=jnp.float32)
        valid = jnp.logical_and(own_head, column < live - start)
        weights = jnp.exp2(jnp.where(valid, scores * scale, NEG))
        total = total + jnp.sum(weights, axis=1, keepdims=True)
        part = part + jnp.dot(
            weights.astype(jnp.bfloat16), values, preferred_element_type=jnp.float32
        )
        return part, total

    part, total = lax.fori_loop(0, (live + chunk - 1) // chunk, step, (part0, total0))
    wide_total = jnp.broadcast_to(total, part.shape)
    for j in range(rows // tree):
        cols = slice(j * head_dim, (j + 1) * head_dim)
        part_ref[:, cols] = part[j * tree : (j + 1) * tree]
        total_ref[:, cols] = wide_total[j * tree : (j + 1) * tree]


def own_attention(queries, cache_keys, cache_values, lengths, tree_keys, tree_values, mask, scale):
    requests, slots, key_heads, head_dim = cache_keys.shape
    rows_local, width = queries.shape
    tree = rows_local // requests
    keys = cache_keys.reshape(requests, slots * key_heads, head_dim)
    values = cache_values.reshape(requests, slots * key_heads, head_dim)
    chunk = 512 * key_heads
    kernel = functools.partial(own_kernel, key_heads, chunk, scale)
    whole = lambda a: pl.BlockSpec((1,) + a.shape[1:], lambda n, _: (n, 0, 0))
    rows_spec = pl.BlockSpec((tree, width), lambda n, _: (n, 0))
    return pl.pallas_call(
        kernel,
        grid_spec=pltpu.PrefetchScalarGridSpec(
            num_scalar_prefetch=1,
            grid=(requests,),
            in_specs=[
                rows_spec, whole(keys), whole(values), whole(tree_keys), whole(tree_values),
                whole(mask),
            ],
            out_specs=[rows_spec, rows_spec],
        ),
        out_shape=[jax.ShapeDtypeStruct((rows_local, width), jnp.float32)] * 2,
        compiler_params=pltpu.CompilerParams(vmem_limit_bytes=40 * 1024 * 1024),
        cost_estimate=pl.CostEstimate(
            flops=8 * rows_local * width * slots * key_heads,
            bytes_accessed=4 * keys.size,
            transcendentals=rows_local * width * slots // 64,
        ),
        name="own_attention",
    )(lengths, queries, keys, values, tree_keys, tree_values, mask)


def prompt_kernel(requests, scale, group_ref, q_ref, *refs):
    key_refs, value_refs, out_ref = refs[0:2], refs[2:4], refs[4]
    step = pl.program_id(0)
    rows, width = q_ref.shape[1:]
    tree = rows // requests
    head_dim = key_refs[0].shape[2]
    heads = width // head_dim
    lanes = heads * tree
    tile_row = lax.broadcasted_iota(jnp.int32, (PAD, lanes), 0)
    totals = jnp.zeros((PAD, lanes), jnp.float32)
    for n in range(requests):
        group = group_ref[step * requests + n]
        query = stack_heads(q_ref[0, n * tree : (n + 1) * tree, :], head_dim)
        part = jnp.zeros((lanes, head_dim), jnp.float32)
        total = jnp.zeros((lanes, 1), jnp.float32)
        for key_ref, value_ref in zip(key_refs, value_refs):
            scores = lax.dot_general(
                query, key_ref[group], CONTRACT_LAST, preferred_element_type=jnp.float32
            )
            weights = jnp.exp2(scores * scale)
            total = total + jnp.sum(weights, axis=1, keepdims=True)
            part = part + jnp.dot(
                weights.astype(jnp.bfloat16), value_ref[group], preferred_element_type=jnp.float32
            )
        turned = jnp.transpose(jnp.broadcast_to(total, (lanes, 128)))[:PAD]
        totals = jnp.where(tile_row == n, turned, totals)
        for j in range(heads):
            out_ref[0, n * tree : (n + 1) * tree, j * head_dim : (j + 1) * head_dim] = part[
                j * tree : (j + 1) * tree
            ].astype(jnp.bfloat16)
    out_ref[0, rows:, :] = jnp.concatenate(
        [totals, jnp.zeros((PAD, width - lanes), jnp.float32)], axis=1
    ).astype(jnp.bfloat16)


def prompt_attention(queries, head, key_heads, groups, keys_pair, values_pair, requests, scale):
    blocks, rows, full = queries.shape
    width = full // key_heads
    whole = lambda a: pl.BlockSpec(a.shape, lambda j, _: (0, 0, 0))
    positions = keys_pair[0].shape[1] * 2
    return pl.pallas_call(
        functools.partial(prompt_kernel, requests, scale),
        grid_spec=pltpu.PrefetchScalarGridSpec(
            num_scalar_prefetch=1,
            grid=(blocks,),
            in_specs=[pl.BlockSpec((1, rows, width), lambda j, _: (j, 0, head))]
            + [whole(a) for a in (*keys_pair, *values_pair)],
            out_specs=pl.BlockSpec((1, rows + PAD, width), lambda j, _: (j, 0, 0)),
        ),
        out_shape=jax.ShapeDtypeStruct((blocks, rows + PAD, width), jnp.bfloat16),
        compiler_params=pltpu.CompilerParams(vmem_limit_bytes=40 * 1024 * 1024),
        cost_estimate=pl.CostEstimate(
            flops=8 * blocks * rows * width * positions,
            bytes_accessed=4 * keys_pair[0].size * 2,
            transcendentals=blocks * rows * width * positions // 128,
        ),
        name="prompt_attention",
    )(groups, queries, *keys_pair, *values_pair)


def add_rounded(left, right):
    return (left.astype(jnp.float32) + right.astype(jnp.float32)).astype(jnp.bfloat16)


def shards(
    n_tok,
    n_mdl,
    tokens,
    norm_gain,
    w_query,
    w_key,
    w_value,
    w_out,
    prompt_keys,
    prompt_values,
    cache_keys,
    cache_values,
    cache_length,
    request_group,
    ancestors,
    accepted,
):
    requests = cache_length.shape[0]
    tree_size = ancestors.shape[1]
    head_dim = prompt_keys.shape[3]
    key_heads = prompt_keys.shape[2]
    query_heads = w_query.shape[1] // head_dim
    group_size = query_heads // key_heads
    scale = head_dim ** (-0.5) * math.log2(math.e)
    rows_local = tokens.shape[0]
    line = n_tok // 2
    swap = [(i, i ^ 1) for i in range(n_tok)]
    tok = lax.axis_index("tok")

    near_keys, near_values, far_keys, far_values = [], [], [], []
    for h in range(key_heads):
        near_keys.append(prompt_keys[:, :, h, :])
        near_values.append(prompt_values[:, :, h, :])
        far_keys.append(lax.ppermute(near_keys[h], "tok", swap))
        far_values.append(lax.ppermute(near_values[h], "tok", swap))

    wide = tokens.astype(jnp.float32)
    normed = (
        wide
        * lax.rsqrt(jnp.mean(wide * wide, axis=1, keepdims=True) + EPS)
        * norm_gain.astype(jnp.float32)
    ).astype(jnp.bfloat16)
    depth = jnp.sum(ancestors, axis=2) - 1
    positions = (PROMPT + cache_length[:, None] + depth).reshape(rows_local)
    queries = jnp.dot(normed, w_query, preferred_element_type=jnp.float32).reshape(
        rows_local, query_heads, head_dim
    )
    queries = (
        rotate_pairs(queries, positions)
        .astype(jnp.bfloat16)
        .reshape(rows_local, query_heads * head_dim)
    )

    def right(value, first, last):
        pairs = [
            (2 * i + y, 2 * (i + 1) + y)
            for i in range(line - 1)
            if first <= i <= last
            for y in range(2)
        ]
        return lax.ppermute(value, "tok", pairs)

    def left(value, first, last):
        pairs = [
            (2 * i + y, 2 * (i - 1) + y)
            for i in range(1, line)
            if first <= i <= last
            for y in range(2)
        ]
        return lax.ppermute(value, "tok", pairs)

    from_left, from_right = [], []
    going_right = going_left = queries
    for s in range(1, line):
        going_right = right(going_right, s - 1, line)
        going_left = left(going_left, 0, line - s)
        from_left.append(going_right)
        from_right.append(going_left)
    place = tok // 2
    blocks = [queries]
    for j in range(1, line):
        blocks.append(jnp.where(place + j < line, from_right[j - 1], from_left[line - j - 1]))
    all_queries = jnp.stack(blocks)
    offsets = jnp.arange(line, dtype=jnp.int32)
    owners = ((place + offsets) % line) * 2 + tok % 2
    groups = jnp.take(request_group.reshape(n_tok, requests), owners, axis=0).reshape(
        line * requests
    )

    new_keys = jnp.dot(normed, w_key, preferred_element_type=jnp.float32).reshape(
        rows_local, key_heads, head_dim
    )
    new_keys = (
        rotate_pairs(new_keys, positions)
        .astype(jnp.bfloat16)
        .reshape(requests, tree_size * key_heads, head_dim)
    )
    new_values = (
        jnp.dot(normed, w_value, preferred_element_type=jnp.float32)
        .astype(jnp.bfloat16)
        .reshape(requests, tree_size * key_heads, head_dim)
    )
    same = jnp.eye(key_heads, dtype=jnp.int32)
    mask = jnp.broadcast_to(
        ancestors[:, None, None, :, :, None] * same[None, :, None, None, None, :],
        (requests, key_heads, group_size, tree_size, tree_size, key_heads),
    ).reshape(requests, query_heads * tree_size, tree_size * key_heads)
    own_part, own_total = own_attention(
        queries, cache_keys, cache_values, cache_length, new_keys, new_values, mask, scale
    )

    merged_heads = []
    width = group_size * head_dim
    for h in range(key_heads):
        messages = prompt_attention(
            all_queries,
            h,
            key_heads,
            groups,
            (near_keys[h], far_keys[h]),
            (near_values[h], far_values[h]),
            requests,
            scale,
        )
        to_right, to_left = messages[line - 1], messages[1 % line]
        for s in range(1, line):
            to_right = right(to_right, 0, s - 1)
            to_left = left(to_left, line - s, line)
            if s < line - 1:
                to_right = add_rounded(messages[line - 1 - s], to_right)
                to_left = add_rounded(messages[s + 1], to_left)
        summed = (
            messages[0].astype(jnp.float32)
            + to_right.astype(jnp.float32)
            + to_left.astype(jnp.float32)
        )
        totals = (
            summed[rows_local : rows_local + requests, : group_size * tree_size]
            .reshape(requests, group_size, tree_size)
            .transpose(0, 2, 1)
            .reshape(rows_local, group_size)
        )
        totals = jnp.broadcast_to(
            totals[:, :, None], (rows_local, group_size, head_dim)
        ).reshape(rows_local, width)
        cols = slice(h * width, (h + 1) * width)
        merged_heads.append(
            (
                (summed[:rows_local] + own_part[:, cols]) / (totals + own_total[:, cols])
            ).astype(jnp.bfloat16)
        )
    attended = jnp.concatenate(merged_heads, axis=1)

    me = lax.axis_index("mdl")
    columns = w_out.shape[1] // n_mdl
    column_start = me * columns
    if n_mdl == 4:
        here, core = me // 2, me % 2

        def project(block):
            piece = lax.dynamic_slice_in_dim(w_out, block * columns, columns, 1)
            return jnp.dot(attended, piece, preferred_element_type=jnp.float32)

        cores = [(i, i ^ 1) for i in range(n_mdl)]
        chips = [(i, i ^ 2) for i in range(n_mdl)]
        far_other = project((1 - here) * 2 + 1 - core).astype(jnp.bfloat16)
        far_other = lax.ppermute(far_other, "mdl", cores)
        far_mine = project((1 - here) * 2 + core)
        far_sum = (far_mine + far_other.astype(jnp.float32)).astype(jnp.bfloat16)
        arrived = lax.ppermute(far_sum, "mdl", chips)
        near_other = project(here * 2 + 1 - core).astype(jnp.bfloat16)
        near_other = lax.ppermute(near_other, "mdl", cores)
        near_mine = project(me)
        attention_out = (
            near_mine + near_other.astype(jnp.float32) + arrived.astype(jnp.float32)
        ).astype(jnp.bfloat16)
    else:
        projected = jnp.dot(attended, w_out, preferred_element_type=jnp.float32)
        attention_out = lax.psum_scatter(
            projected.astype(jnp.bfloat16), "mdl", scatter_dimension=1, tiled=True
        )
    residual = lax.dynamic_slice_in_dim(tokens, column_start, columns, 1).astype(
        jnp.float32
    ) + attention_out.astype(jnp.float32)
    rows_index = (
        jnp.arange(requests, dtype=jnp.int32)[:, None] * tree_size + jnp.maximum(accepted, 0)
    ).reshape(requests * accepted.shape[1])
    picked = jnp.take(residual, rows_index, axis=0).reshape(requests, accepted.shape[1], columns)
    compact_rows = jnp.where(accepted[:, :, None] >= 0, picked, 0.0).astype(jnp.bfloat16)
    return (attention_out, compact_rows)


def solution(mesh):
    placed = (
        P("tok", None),
        P(),
        P(None, "mdl"),
        P(None, "mdl"),
        P(None, "mdl"),
        P("mdl", None),
        P(None, "tok", "mdl", None),
        P(None, "tok", "mdl", None),
        P("tok", None, "mdl", None),
        P("tok", None, "mdl", None),
        P("tok"),
        P(),
        P("tok", None, None),
        P("tok", None),
    )
    return jax.shard_map(
        functools.partial(shards, mesh.shape["tok"], mesh.shape["mdl"]),
        mesh=mesh,
        in_specs=placed,
        out_specs=(P("tok", "mdl"), P("tok", None, "mdl")),
        check_vma=False,
    )
```

```python
import functools
import math

import jax
import jax.numpy as jnp
from jax import lax
from jax.experimental import pallas as pl
from jax.experimental.pallas import tpu as pltpu
from jax.sharding import PartitionSpec as P

PROMPT = 4096
THETA = 100000000.0
EPS = 1e-05
PAD = 16
NEG = -1e30
CONTRACT_LAST = (((1,), (1,)), ((), ()))


def rotate_pairs(vectors, positions):
    middle = vectors.shape[-1] // 2
    exponent = jnp.arange(middle, dtype=jnp.float32) * (2.0 / vectors.shape[-1])
    inverse = jnp.power(jnp.float32(THETA), -exponent)
    angles = positions.astype(jnp.float32)[:, None] * inverse[None, :]
    cosine = jnp.cos(angles)[:, None, :]
    sine_part = jnp.sin(angles)[:, None, :]
    leading = vectors[..., :middle]
    trailing = vectors[..., middle:]
    return jnp.concatenate(
        [leading * cosine - trailing * sine_part, trailing * cosine + leading * sine_part], axis=-1
    )


def stack_heads(block, head_dim):
    count = block.shape[1] // head_dim
    return jnp.concatenate(
        [block[:, j * head_dim : (j + 1) * head_dim] for j in range(count)], axis=0
    )


def own_kernel(
    key_heads, chunk, scale, length_ref, q_ref, k_ref, v_ref, tk_ref, tv_ref, mask_ref,
    part_ref, total_ref,
):
    n = pl.program_id(0)
    tree, width = q_ref.shape
    head_dim = k_ref.shape[2]
    query = stack_heads(q_ref[...], head_dim)
    rows = query.shape[0]
    per = rows // key_heads
    live = length_ref[n] * key_heads

    tree_keys = stack_heads(tk_ref[...], head_dim)
    tree_values = stack_heads(tv_ref[...], head_dim)
    lineage = jnp.concatenate([mask_ref[0]] * (rows // tree), axis=0)
    tree_row = lax.broadcasted_iota(jnp.int32, lineage.shape, 0) // per
    tree_column = lax.broadcasted_iota(jnp.int32, lineage.shape, 1) // tree
    scores = lax.dot_general(query, tree_keys, CONTRACT_LAST, preferred_element_type=jnp.float32)
    allowed = jnp.logical_and(lineage > 0, tree_row == tree_column)
    weights = jnp.exp2(jnp.where(allowed, scores * scale, NEG))
    total0 = jnp.sum(weights, axis=1, keepdims=True)
    part0 = jnp.dot(weights.astype(jnp.bfloat16), tree_values, preferred_element_type=jnp.float32)
    row_head = lax.broadcasted_iota(jnp.int32, (rows, chunk), 0) // per
    column = lax.broadcasted_iota(jnp.int32, (rows, chunk), 1)
    own_head = (column % key_heads) == row_head

    def step(i, carry):
        part, total = carry
        start = pl.multiple_of(i * chunk, chunk)
        keys = k_ref[0, pl.ds(start, chunk), :]
        values = v_ref[0, pl.ds(start, chunk), :]
        scores = lax.dot_general(query, keys, CONTRACT_LAST, preferred_element_type=jnp.float32)
        valid = jnp.logical_and(own_head, column < live - start)
        weights = jnp.exp2(jnp.where(valid, scores * scale, NEG))
        total = total + jnp.sum(weights, axis=1, keepdims=True)
        part = part + jnp.dot(
            weights.astype(jnp.bfloat16), values, preferred_element_type=jnp.float32
        )
        return part, total

    part, total = lax.fori_loop(0, (live + chunk - 1) // chunk, step, (part0, total0))
    wide_total = jnp.broadcast_to(total, part.shape)
    for j in range(rows // tree):
        cols = slice(j * head_dim, (j + 1) * head_dim)
        part_ref[:, cols] = part[j * tree : (j + 1) * tree]
        total_ref[:, cols] = wide_total[j * tree : (j + 1) * tree]


def own_attention(queries, cache_keys, cache_values, lengths, tree_keys, tree_values, mask, scale):
    requests, slots, key_heads, head_dim = cache_keys.shape
    rows_local, width = queries.shape
    tree = rows_local // requests
    keys = cache_keys.reshape(requests, slots * key_heads, head_dim)
    values = cache_values.reshape(requests, slots * key_heads, head_dim)
    chunk = 512 * key_heads
    kernel = functools.partial(own_kernel, key_heads, chunk, scale)
    whole = lambda a: pl.BlockSpec((1,) + a.shape[1:], lambda n, _: (n, 0, 0))
    rows_spec = pl.BlockSpec((tree, width), lambda n, _: (n, 0))
    tree_spec = pl.BlockSpec((tree, tree_keys.shape[1]), lambda n, _: (n, 0))
    return pl.pallas_call(
        kernel,
        grid_spec=pltpu.PrefetchScalarGridSpec(
            num_scalar_prefetch=1,
            grid=(requests,),
            in_specs=[
                rows_spec, whole(keys), whole(values), tree_spec, tree_spec, whole(mask),
            ],
            out_specs=[rows_spec, rows_spec],
        ),
        out_shape=[jax.ShapeDtypeStruct((rows_local, width), jnp.float32)] * 2,
        compiler_params=pltpu.CompilerParams(vmem_limit_bytes=40 * 1024 * 1024),
        cost_estimate=pl.CostEstimate(
            flops=8 * rows_local * width * slots * key_heads,
            bytes_accessed=4 * keys.size,
            transcendentals=rows_local * width * slots // 64,
        ),
        name="own_attention",
    )(lengths, queries, keys, values, tree_keys, tree_values, mask)


def prompt_kernel(requests, scale, group_ref, q_ref, *refs):
    pair, out_ref = refs[:2], refs[2]
    group_count = pair[0].shape[0] // 2
    step = pl.program_id(0)
    rows, width = q_ref.shape[1:]
    tree = rows // requests
    head_dim = pair[0].shape[2]
    heads = width // head_dim
    lanes = heads * tree
    tile_row = lax.broadcasted_iota(jnp.int32, (PAD, lanes), 0)
    totals = jnp.zeros((PAD, lanes), jnp.float32)
    for n in range(requests):
        group = group_ref[step * requests + n]
        query = stack_heads(q_ref[0, n * tree : (n + 1) * tree, :], head_dim)
        part = jnp.zeros((lanes, head_dim), jnp.float32)
        total = jnp.zeros((lanes, 1), jnp.float32)
        for prompt_ref in pair:
            scores = lax.dot_general(
                query, prompt_ref[group], CONTRACT_LAST, preferred_element_type=jnp.float32
            )
            weights = jnp.exp2(scores * scale)
            total = total + jnp.sum(weights, axis=1, keepdims=True)
            part = part + jnp.dot(
                weights.astype(jnp.bfloat16),
                prompt_ref[group_count + group],
                preferred_element_type=jnp.float32,
            )
        turned = jnp.transpose(jnp.broadcast_to(total, (lanes, 128)))[:PAD]
        totals = jnp.where(tile_row == n, turned, totals)
        for j in range(heads):
            out_ref[0, n * tree : (n + 1) * tree, j * head_dim : (j + 1) * head_dim] = part[
                j * tree : (j + 1) * tree
            ].astype(jnp.bfloat16)
    out_ref[0, rows:, :] = jnp.concatenate(
        [totals, jnp.zeros((PAD, width - lanes), jnp.float32)], axis=1
    ).astype(jnp.bfloat16)


def prompt_attention(queries, head, key_heads, groups, pair, requests, scale):
    blocks, rows, full = queries.shape
    width = full // key_heads
    whole = lambda a: pl.BlockSpec(a.shape, lambda j, _: (0, 0, 0))
    positions = pair[0].shape[1] * 2
    return pl.pallas_call(
        functools.partial(prompt_kernel, requests, scale),
        grid_spec=pltpu.PrefetchScalarGridSpec(
            num_scalar_prefetch=1,
            grid=(blocks,),
            in_specs=[pl.BlockSpec((1, rows, width), lambda j, _: (j, 0, head))]
            + [whole(a) for a in pair],
            out_specs=pl.BlockSpec((1, rows + PAD, width), lambda j, _: (j, 0, 0)),
        ),
        out_shape=jax.ShapeDtypeStruct((blocks, rows + PAD, width), jnp.bfloat16),
        compiler_params=pltpu.CompilerParams(vmem_limit_bytes=40 * 1024 * 1024),
        cost_estimate=pl.CostEstimate(
            flops=8 * blocks * rows * width * positions,
            bytes_accessed=4 * pair[0].size,
            transcendentals=blocks * rows * width * positions // 128,
        ),
        name="prompt_attention",
    )(groups, queries, *pair)


def add_rounded(left, right):
    return (left.astype(jnp.float32) + right.astype(jnp.float32)).astype(jnp.bfloat16)


def shards(
    n_tok,
    n_mdl,
    tokens,
    norm_gain,
    w_query,
    w_key,
    w_value,
    w_out,
    prompt_keys,
    prompt_values,
    cache_keys,
    cache_values,
    cache_length,
    request_group,
    ancestors,
    accepted,
):
    requests = cache_length.shape[0]
    tree_size = ancestors.shape[1]
    head_dim = prompt_keys.shape[3]
    key_heads = prompt_keys.shape[2]
    query_heads = w_query.shape[1] // head_dim
    group_size = query_heads // key_heads
    scale = head_dim ** (-0.5) * math.log2(math.e)
    rows_local = tokens.shape[0]
    line = n_tok // 2
    swap = [(i, i ^ 1) for i in range(n_tok)]
    tok = lax.axis_index("tok")

    near = [
        jnp.concatenate([prompt_keys[:, :, h, :], prompt_values[:, :, h, :]], axis=0)
        for h in range(key_heads)
    ]
    tokens, near = lax.optimization_barrier((tokens, near))
    far = [lax.ppermute(piece, "tok", swap) for piece in near]

    wide = tokens.astype(jnp.float32)
    normed = (
        wide
        * lax.rsqrt(jnp.mean(wide * wide, axis=1, keepdims=True) + EPS)
        * norm_gain.astype(jnp.float32)
    ).astype(jnp.bfloat16)
    depth = jnp.sum(ancestors, axis=2) - 1
    positions = (PROMPT + cache_length[:, None] + depth).reshape(rows_local)
    queries = jnp.dot(normed, w_query, preferred_element_type=jnp.float32).reshape(
        rows_local, query_heads, head_dim
    )
    queries = (
        rotate_pairs(queries, positions)
        .astype(jnp.bfloat16)
        .reshape(rows_local, query_heads * head_dim)
    )

    def right(value, first, last):
        pairs = [
            (2 * i + y, 2 * (i + 1) + y)
            for i in range(line - 1)
            if first <= i <= last
            for y in range(2)
        ]
        return lax.ppermute(value, "tok", pairs)

    def left(value, first, last):
        pairs = [
            (2 * i + y, 2 * (i - 1) + y)
            for i in range(1, line)
            if first <= i <= last
            for y in range(2)
        ]
        return lax.ppermute(value, "tok", pairs)

    from_left, from_right = [], []
    going_right = going_left = queries
    for s in range(1, line):
        going_right = right(going_right, s - 1, line)
        going_left = left(going_left, 0, line - s)
        from_left.append(going_right)
        from_right.append(going_left)
    place = tok // 2
    blocks = [queries]
    for j in range(1, line):
        blocks.append(jnp.where(place + j < line, from_right[j - 1], from_left[line - j - 1]))
    all_queries = jnp.stack(blocks)
    offsets = jnp.arange(line, dtype=jnp.int32)
    owners = ((place + offsets) % line) * 2 + tok % 2
    groups = jnp.take(request_group.reshape(n_tok, requests), owners, axis=0).reshape(
        line * requests
    )

    new_keys = jnp.dot(normed, w_key, preferred_element_type=jnp.float32).reshape(
        rows_local, key_heads, head_dim
    )
    new_keys = (
        rotate_pairs(new_keys, positions)
        .astype(jnp.bfloat16)
        .reshape(rows_local, key_heads * head_dim)
    )
    new_values = jnp.dot(normed, w_value, preferred_element_type=jnp.float32).astype(jnp.bfloat16)
    mask = jnp.concatenate([ancestors] * key_heads, axis=2)
    own_part, own_total = own_attention(
        queries, cache_keys, cache_values, cache_length, new_keys, new_values, mask, scale
    )

    all_queries, own_part, own_total = lax.optimization_barrier((all_queries, own_part, own_total))

    merged_heads = []
    width = group_size * head_dim
    for h in range(key_heads):
        messages = prompt_attention(
            all_queries,
            h,
            key_heads,
            groups,
            (near[h], far[h]),
            requests,
            scale,
        )
        to_right, to_left = messages[line - 1], messages[1 % line]
        for s in range(1, line):
            to_right = right(to_right, 0, s - 1)
            to_left = left(to_left, line - s, line)
            if s < line - 1:
                to_right = add_rounded(messages[line - 1 - s], to_right)
                to_left = add_rounded(messages[s + 1], to_left)
        summed = (
            messages[0].astype(jnp.float32)
            + to_right.astype(jnp.float32)
            + to_left.astype(jnp.float32)
        )
        totals = (
            summed[rows_local : rows_local + requests, : group_size * tree_size]
            .reshape(requests, group_size, tree_size)
            .transpose(0, 2, 1)
            .reshape(rows_local, group_size)
        )
        totals = jnp.broadcast_to(
            totals[:, :, None], (rows_local, group_size, head_dim)
        ).reshape(rows_local, width)
        cols = slice(h * width, (h + 1) * width)
        merged_heads.append(
            (
                (summed[:rows_local] + own_part[:, cols]) / (totals + own_total[:, cols])
            ).astype(jnp.bfloat16)
        )

    me = lax.axis_index("mdl")
    columns = w_out.shape[1] // n_mdl
    column_start = me * columns
    if n_mdl == 4:
        here, core = me // 2, me % 2

        def project(block):
            piece = lax.dynamic_slice_in_dim(w_out, block * columns, columns, 1)
            return sum(
                jnp.dot(
                    part,
                    piece[h * width : (h + 1) * width],
                    preferred_element_type=jnp.float32,
                )
                for h, part in enumerate(merged_heads)
            )

        cores = [(i, i ^ 1) for i in range(n_mdl)]
        chips = [(i, i ^ 2) for i in range(n_mdl)]
        far_other = project((1 - here) * 2 + 1 - core).astype(jnp.bfloat16)
        far_other = lax.ppermute(far_other, "mdl", cores)
        far_mine = project((1 - here) * 2 + core)
        far_sum = (far_mine + far_other.astype(jnp.float32)).astype(jnp.bfloat16)
        arrived = lax.ppermute(far_sum, "mdl", chips)
        near_other = project(here * 2 + 1 - core).astype(jnp.bfloat16)
        near_other = lax.ppermute(near_other, "mdl", cores)
        near_mine = project(me)
        attention_out = (
            near_mine + near_other.astype(jnp.float32) + arrived.astype(jnp.float32)
        ).astype(jnp.bfloat16)
    else:
        attended = jnp.concatenate(merged_heads, axis=1)
        projected = jnp.dot(attended, w_out, preferred_element_type=jnp.float32)
        attention_out = lax.psum_scatter(
            projected.astype(jnp.bfloat16), "mdl", scatter_dimension=1, tiled=True
        )
    residual = lax.dynamic_slice_in_dim(tokens, column_start, columns, 1).astype(
        jnp.float32
    ) + attention_out.astype(jnp.float32)
    rows_index = (
        jnp.arange(requests, dtype=jnp.int32)[:, None] * tree_size + jnp.maximum(accepted, 0)
    ).reshape(requests * accepted.shape[1])
    picked = jnp.take(residual, rows_index, axis=0).reshape(requests, accepted.shape[1], columns)
    compact_rows = jnp.where(accepted[:, :, None] >= 0, picked, 0.0).astype(jnp.bfloat16)
    return (attention_out, compact_rows)


def solution(mesh):
    placed = (
        P("tok", None),
        P(),
        P(None, "mdl"),
        P(None, "mdl"),
        P(None, "mdl"),
        P("mdl", None),
        P(None, "tok", "mdl", None),
        P(None, "tok", "mdl", None),
        P("tok", None, "mdl", None),
        P("tok", None, "mdl", None),
        P("tok"),
        P(),
        P("tok", None, None),
        P("tok", None),
    )
    return jax.shard_map(
        functools.partial(shards, mesh.shape["tok"], mesh.shape["mdl"]),
        mesh=mesh,
        in_specs=placed,
        out_specs=(P("tok", "mdl"), P("tok", None, "mdl")),
        check_vma=False,
    )
```
